32 devices in a mesh: dp: 8 (over y, x, core), mp: 4 (over z).
Axes of the slice: x: 2, y: 2, z: 4, core: 2. Of those that a mesh axis runs over, the one named last changes fastest.
Arguments:
- inputs: float32 [8192, 768], P(('dp', 'mp')), may hold values from -6 to 6
- cotangent: float32 [8192, 768], P(('dp', 'mp')), may hold values from -0.5 to 0.5
- loss_mask: int32 [8192], P(('dp', 'mp')), may hold values from 0 to 1, as said below
- keep_mask: int32 [8], P('dp'), may hold values 0 or 1
- w_qkv: float32 [2, 3, 768, 768], P(None, None, None, 'mp'), may hold values from -0.21875 to 0.21875
- w_out: float32 [2, 768, 768], P(None, 'mp'), may hold values from -1.75 to 1.75
- w_in: float32 [2, 768, 3072], P(None, None, 'mp'), may hold values from -0.21875 to 0.21875
- w_down: float32 [2, 3072, 768], P(None, 'mp'), may hold values from -0.109375 to 0.109375
- norm_params: float32 [2, 2, 2, 768], replicated, may hold values from -1 to 1.5, as said below
- norm_moments: float32 [2, 2, 2, 768], replicated, may hold values from 0.11 to 0.45
- left_stats: float32 [1536, 96, 96], P(('dp', 'mp')), may hold values from -8 to 43, as said below
- right_stats: float32 [1536, 96, 96], P(('dp', 'mp')), may hold values from -8 to 43, as said below
- left_roots: float32 [1536, 96, 96], P(('dp', 'mp')), may hold values from -1 to 2, as said below
- right_roots: float32 [1536, 96, 96], P(('dp', 'mp')), may hold values from -1 to 2, as said below
Outputs:
- outputs: float32 [8192, 768], P(('dp', 'mp'))
- in_grads: float32 [8192, 768], P(('dp', 'mp'))
- block_grads: float32 [1536, 96, 96], P(('dp', 'mp'))
- left_new: float32 [1536, 96, 96], P(('dp', 'mp'))
- right_new: float32 [1536, 96, 96], P(('dp', 'mp'))
- qkv_new: float32 [2, 3, 768, 768], P(None, None, None, 'mp')
- out_new: float32 [2, 768, 768], P(None, 'mp')
- in_new: float32 [2, 768, 3072], P(None, None, 'mp')
- down_new: float32 [2, 3072, 768], P(None, 'mp')
- norm_grads: float32 [2, 2, 2, 768], replicated
- moments_new: float32 [2, 2, 2, 768], replicated
- norms_new: float32 [2, 2, 2, 768], replicated
The draws below stay inside these ranges and needn't reach their ends.
Inputs may be any that keep to these rules, and one draw needn't show every extreme that they name: `loss_mask`: each sequence's tokens are 1 with a chance of 5 to 25 percent drawn for that sequence. `norm_params`: gains near 1, biases near 0. `left_stats`: each block is symmetric. `right_stats`: each block is symmetric. `left_roots`: each block is symmetric. `right_roots`: each block is symmetric.
All inputs are finite; a program needn't handle non-finite values. No bound on the sum of `keep_mask` on one device may be relied on, other than what follows from the above.
Results may differ from the reference program's by a relative error of at most 0.0003.
Values sent between devices are 32-bit elements; how exact they have to be, the bound alone decides.
A program may use at most 256 MiB of HBM per device.

```python
import math
import jax
import jax.numpy as jnp
from jax import lax

D = 768
HEADS = 12
HEAD = 64
FF = 3072
LEN = 1024
LAYERS = 2
BLOCK = 96
SEQS = 8
TOKENS = 8192
BLK_LAYER = 192
BPL = 24
BLOCKS = 1536
N_DP = 8
N_MP = 4


def symmetric_blocks(key, diag_lo, diag_hi, off_scale):
    key_diag, key_off = jax.random.split(key)
    diagonal = jnp.exp(jax.random.uniform(key_diag, (BLOCKS, BLOCK), jnp.float32, jnp.log(diag_lo), jnp.log(diag_hi)))
    noise = jnp.clip(jax.random.normal(key_off, (BLOCKS, BLOCK, BLOCK), jnp.float32), -5.0, 5.0)
    mirrored = (noise + jnp.swapaxes(noise, 1, 2)) * (off_scale * 0.7071)
    identity = jnp.eye(BLOCK, dtype=jnp.float32)
    return mirrored * (1.0 - identity) + diagonal[:, :, None] * identity


def draw_loss_mask(key, part):
    key = jax.random.fold_in(key, 11)
    key_rate, key_pick = jax.random.split(key)
    factors = jax.random.randint(key_rate, (3, SEQS), 0, 21)
    percent = 5 + factors[0] * factors[1] * factors[2] // 400
    chance = jax.random.randint(key_pick, (SEQS, LEN), 0, 100)
    return (chance < percent[:, None]).astype(jnp.int32).reshape(TOKENS)


def draw_norm_params(key, part):
    key = jax.random.fold_in(key, 5)
    noise = jnp.clip(jax.random.normal(key, (LAYERS, 2, 2, D), jnp.float32), -5.0, 5.0)
    spreads = jnp.array([0.1, 0.2], jnp.float32)[:, None]
    centers = jnp.array([1.0, 0.0], jnp.float32)[:, None]
    return noise * spreads + centers


def draw_left_stats(key, part):
    key = jax.random.fold_in(key, 21)
    return symmetric_blocks(key, BLOCK / 9.0, 4.0 * BLOCK / 9.0, BLOCK ** 0.5 / 9.0)


def draw_right_stats(key, part):
    key = jax.random.fold_in(key, 22)
    return symmetric_blocks(key, BLOCK / 9.0, 4.0 * BLOCK / 9.0, BLOCK ** 0.5 / 9.0)


def draw_left_roots(key, part):
    key = jax.random.fold_in(key, 31)
    return symmetric_blocks(key, 0.5, 2.0, 0.3 * BLOCK ** (-0.5))


def draw_right_roots(key, part):
    key = jax.random.fold_in(key, 32)
    return symmetric_blocks(key, 0.5, 2.0, 0.3 * BLOCK ** (-0.5))


def touch_ends(values, stream_key, low, high):
    dims = values.shape
    spot = [jax.random.randint(jax.random.fold_in(stream_key, axis), (), 0, dims[axis]) for axis in range(len(dims))]
    values = values.at[tuple(spot)].set(low)
    longest = dims.index(max(dims))
    spot[longest] = (spot[longest] + 1) % dims[longest]
    return values.at[tuple(spot)].set(high)


def levels(rng, extent, shards, least, top_value):
    loudness = 1.0
    for dim, parts in shards:
        heights = jax.random.uniform(jax.random.fold_in(jax.random.fold_in(rng, 6), dim), (parts,), jnp.float32, least / len(shards), top_value / len(shards))
        loudness = loudness * jnp.repeat(jnp.exp(heights), extent[dim] // parts).reshape((-1,) + (1,) * (len(extent) - 1 - dim))
    return loudness


def gaussian(stream_key, extent, scale, limit, cuts=(), held_as=jnp.bfloat16):
    result = jax.random.normal(stream_key, extent, jnp.float32) * scale
    if len(cuts) > 0:
        result = levels(stream_key, extent, cuts, -0.22, 0.18) * result
    return jnp.clip(result, min=-limit, max=limit).astype(held_as)


def setup_inputs(seed: int = 0) -> dict:
    arg_keys = jax.random.split(jax.random.key(seed), 15)
    return {
        "inputs": gaussian(arg_keys[0], (TOKENS, D), 1.0, 6.0, ((0, 32),), jnp.float32),
        "cotangent": gaussian(arg_keys[1], (TOKENS, D), (3 * TOKENS ** -0.5), 0.5, ((0, 32),), jnp.float32),
        "loss_mask": draw_loss_mask(jax.random.fold_in(arg_keys[14], 71), 0),
        "keep_mask": touch_ends((jax.random.randint(arg_keys[3], (SEQS,), 0, 4) < 3).astype(jnp.int32), jax.random.fold_in(arg_keys[3], 1), 0, 1),
        "w_qkv": gaussian(arg_keys[4], (LAYERS, 3, D, D), D ** -0.5, 0.21875, ((3, 4),), jnp.float32),
        "w_out": gaussian(arg_keys[5], (LAYERS, D, D), (max(1, D * 16 // LEN)) ** -0.5, 1.75, ((1, 4),), jnp.float32),
        "w_in": gaussian(arg_keys[6], (LAYERS, D, FF), D ** -0.5, 0.21875, ((2, 4),), jnp.float32),
        "w_down": gaussian(arg_keys[7], (LAYERS, FF, D), FF ** -0.5, 0.109375, ((1, 4),), jnp.float32),
        "norm_params": draw_norm_params(jax.random.fold_in(arg_keys[14], 71), 0),
        "norm_moments": jnp.clip(jnp.exp(jax.random.uniform(arg_keys[9], (LAYERS, 2, 2, D), jnp.float32, math.log(0.11), math.log(0.45))), 0.11, 0.45),
        "left_stats": draw_left_stats(jax.random.fold_in(arg_keys[14], 71), 0),
        "right_stats": draw_right_stats(jax.random.fold_in(arg_keys[14], 71), 0),
        "left_roots": draw_left_roots(jax.random.fold_in(arg_keys[14], 71), 0),
        "right_roots": draw_right_roots(jax.random.fold_in(arg_keys[14], 71), 0),
    }


@jax.custom_vjp
def low(v):
    return lax.optimization_barrier(v.astype(jnp.bfloat16)).astype(jnp.float32)

@jax.custom_vjp
def low_back(v):
    return v

def low_keep(v):
    return (low(v), None)

def low_pass(kept, grad):
    return (grad,)

def back_keep(v):
    return (v, None)

def back_low(kept, grad):
    return (low(grad),)
low.defvjp(low_keep, low_pass)
low_back.defvjp(back_keep, back_low)
HIGHEST = lax.Precision.HIGHEST
norm_eps = 1e-05
stat_decay = 0.9
shampoo_rate = 0.02
graft_eps = 1e-06
moment_decay = 0.9
vector_rate = 0.05
vector_eps = 1e-08

def layer_norm(hidden, gain_vec, bias_vec):
    center = lax.optimization_barrier(jnp.mean(hidden, axis=-1, keepdims=True))
    shifted = hidden - center
    spread = lax.optimization_barrier(jnp.mean(shifted * shifted, axis=-1, keepdims=True))
    return shifted * lax.rsqrt(spread + norm_eps) * gain_vec + bias_vec

def encoder_layer(seq_rows, qkv_layer, out_layer, in_layer, down_layer, norm_set):
    queries = jnp.dot(seq_rows, qkv_layer[0], precision=HIGHEST).reshape(LEN, HEADS, HEAD)
    key_rows = jnp.dot(seq_rows, qkv_layer[1], precision=HIGHEST).reshape(LEN, HEADS, HEAD)
    value_rows = jnp.dot(seq_rows, qkv_layer[2], precision=HIGHEST).reshape(LEN, HEADS, HEAD)
    scores = jnp.einsum('qhd,khd->hqk', queries, key_rows, precision=HIGHEST) * HEAD ** (-0.5)
    attn_probs = jax.nn.softmax(scores, axis=-1)
    context = jnp.einsum('hqk,khd->qhd', attn_probs, value_rows, precision=HIGHEST).reshape(LEN, D)
    attn_sum = seq_rows + jnp.dot(context, out_layer, precision=HIGHEST)
    middle = layer_norm(attn_sum, norm_set[0, 0], norm_set[0, 1])
    activated = jax.nn.gelu(jnp.dot(middle, in_layer, precision=HIGHEST), approximate=False)
    second_sum = middle + jnp.dot(activated, down_layer, precision=HIGHEST)
    return layer_norm(second_sum, norm_set[1, 0], norm_set[1, 1])

def network(param_set, seq_rows, keep_flag):
    qkv_all, out_all, in_all, down_all, norm_all = param_set
    first_out = encoder_layer(seq_rows, qkv_all[0], out_all[0], in_all[0], down_all[0], norm_all[0])
    second = encoder_layer(first_out, qkv_all[1], out_all[1], in_all[1], down_all[1], norm_all[1])
    return first_out + keep_flag * (second - first_out)

def cut_blocks(matrix):
    leading = tuple(matrix.shape[:-2])
    row_count, col_count = matrix.shape[-2:]
    tiled = matrix.reshape(leading + (row_count // BLOCK, BLOCK, col_count // BLOCK, BLOCK))
    return jnp.swapaxes(tiled, -3, -2).reshape(-1, BLOCK, BLOCK)

def tile_blocks(qkv_part, out_part, in_part, down_part):
    return jnp.concatenate([cut_blocks(qkv_part), cut_blocks(out_part), cut_blocks(in_part), cut_blocks(down_part)], axis=0)

def join_blocks(blocks, target_shape):
    leading = tuple(target_shape[:-2])
    row_count, col_count = target_shape[-2:]
    tiled = blocks.reshape(leading + (row_count // BLOCK, col_count // BLOCK, BLOCK, BLOCK))
    return jnp.swapaxes(tiled, -3, -2).reshape(target_shape)

def untile_blocks(blocks, shape_list):
    pieces = []
    offset = 0
    for target_shape in shape_list:
        block_count = math.prod(target_shape) // (BLOCK * BLOCK)
        pieces.append(join_blocks(blocks[offset:offset + block_count], target_shape))
        offset = offset + block_count
    return pieces

def global_blocks(qkv_all, out_all, in_all, down_all):
    width_loc = D // N_MP
    hidden_loc = FF // N_MP
    layer_list = []
    for layer_idx in range(LAYERS):
        piece_list = []
        for member in range(N_MP):
            low_col = member * width_loc
            low_unit = member * hidden_loc
            piece_list.append(tile_blocks(qkv_all[layer_idx][:, :, low_col:low_col + width_loc], out_all[layer_idx][low_col:low_col + width_loc], in_all[layer_idx][:, low_unit:low_unit + hidden_loc], down_all[layer_idx][low_unit:low_unit + hidden_loc]))
        layer_list.append(jnp.stack(piece_list))
    stacked = jnp.stack(layer_list).reshape(LAYERS, N_MP, N_DP, BPL, BLOCK, BLOCK)
    return jnp.transpose(stacked, (2, 1, 0, 3, 4, 5)).reshape(BLOCKS, BLOCK, BLOCK)

def global_weights(blocks):
    width_loc = D // N_MP
    hidden_loc = FF // N_MP
    arranged = jnp.transpose(blocks.reshape(N_DP, N_MP, LAYERS, BPL, BLOCK, BLOCK), (2, 1, 0, 3, 4, 5))
    arranged = arranged.reshape(LAYERS, N_MP, BLK_LAYER, BLOCK, BLOCK)
    shape_list = [(3, D, width_loc), (width_loc, D), (D, hidden_loc), (hidden_loc, D)]
    qkv_layers, out_layers, in_layers, down_layers = ([], [], [], [])
    for layer_idx in range(LAYERS):
        member_sets = [untile_blocks(arranged[layer_idx, member], shape_list) for member in range(N_MP)]
        qkv_layers.append(jnp.concatenate([piece_set[0] for piece_set in member_sets], axis=2))
        out_layers.append(jnp.concatenate([piece_set[1] for piece_set in member_sets], axis=0))
        in_layers.append(jnp.concatenate([piece_set[2] for piece_set in member_sets], axis=1))
        down_layers.append(jnp.concatenate([piece_set[3] for piece_set in member_sets], axis=0))
    return (jnp.stack(qkv_layers), jnp.stack(out_layers), jnp.stack(in_layers), jnp.stack(down_layers))

def reference(inputs, cotangent, loss_mask, keep_mask, w_qkv, w_out, w_in, w_down, norm_params, norm_moments, left_stats, right_stats, left_roots, right_roots):
    seq_inputs = inputs.reshape(SEQS, LEN, D)
    masked_grad = (cotangent * loss_mask.astype(jnp.float32)[:, None]).reshape(SEQS, LEN, D)
    param_set = (w_qkv, w_out, w_in, w_down, norm_params)
    zero_sums = jax.tree.map(jnp.zeros_like, param_set)

    def single_seq(grad_sums, seq_item):
        seq_rows, seq_back, keep_flag = seq_item
        seq_out, pullback = jax.vjp(lambda params_now, rows_now: network(params_now, rows_now, keep_flag), param_set, seq_rows)
        param_grads, row_grads = pullback(seq_back)
        return (jax.tree.map(jnp.add, grad_sums, param_grads), (seq_out, row_grads))
    grad_sums, (seq_outs, seq_grads) = lax.scan(single_seq, zero_sums, (seq_inputs, masked_grad, keep_mask.astype(jnp.float32)))
    grad_qkv, grad_out, grad_in, grad_down, norm_grads = grad_sums
    block_grads = global_blocks(grad_qkv, grad_out, grad_in, grad_down)
    left_new = stat_decay * left_stats + (1.0 - stat_decay) * jnp.einsum('nij,nkj->nik', block_grads, block_grads, precision=HIGHEST)
    right_new = stat_decay * right_stats + (1.0 - stat_decay) * jnp.einsum('nji,njk->nik', block_grads, block_grads, precision=HIGHEST)
    right_side = jnp.einsum('nij,njk->nik', block_grads, right_roots, precision=HIGHEST)
    precond = jnp.einsum('nij,njk->nik', left_roots, right_side, precision=HIGHEST)
    old_blocks = global_blocks(w_qkv, w_out, w_in, w_down)
    renewed = old_blocks - shampoo_rate * precond * lax.rsqrt(lax.optimization_barrier(jnp.mean(precond * precond, axis=(1, 2), keepdims=True)) + graft_eps)
    qkv_new, out_new, in_new, down_new = global_weights(renewed)
    moments_new = moment_decay * norm_moments + (1.0 - moment_decay) * norm_grads * norm_grads
    norms_new = norm_params - vector_rate * norm_grads / (jnp.sqrt(moments_new) + vector_eps)
    return (seq_outs.reshape(TOKENS, D), seq_grads.reshape(TOKENS, D), block_grads, left_new, right_new, qkv_new, out_new, in_new, down_new, norm_grads, moments_new, norms_new)
```

```python
import functools
import math

import jax
import jax.numpy as jnp
from jax import lax
from jax.experimental import pallas as pl
from jax.experimental.pallas import tpu as pltpu
from jax.sharding import Mesh, PartitionSpec as P

HEAD = 64
LEN = 1024
BLOCK = 96


HIGHEST = lax.Precision.HIGHEST
norm_eps = 1e-05
stat_decay = 0.9
shampoo_rate = 0.02
graft_eps = 1e-06
moment_decay = 0.9
vector_rate = 0.05
vector_eps = 1e-08
sqrt_half = 0.7071067811865476
inv_sqrt_tau = 0.3989422804014327


def matmul(left_op, right_op):
    return jnp.dot(left_op, right_op, precision=HIGHEST)


def matmul_t(left_op, right_op):
    return jnp.einsum("sa,ba->sb", left_op, right_op, precision=HIGHEST)


def inner_rows(left_op, right_op):
    return jnp.einsum("sa,sb->ab", left_op, right_op, precision=HIGHEST)


def gather_rows(local_rows):
    return lax.all_gather(local_rows, "mp", axis=0, tiled=True)


def reduce_rows(partial_value):
    return lax.psum_scatter(partial_value, "mp", scatter_dimension=0, tiled=True)


def gather_grads(local_rows):
    return lax.all_gather(local_rows, "mp", axis=0, tiled=True)


def reduce_grads(partial_value):
    return lax.psum_scatter(partial_value, "mp", scatter_dimension=0, tiled=True)


def norm_forward(hidden, gain_vec, bias_vec):
    center = jnp.mean(hidden, axis=-1, keepdims=True)
    shifted = hidden - center
    spread = jnp.mean(shifted * shifted, axis=-1, keepdims=True)
    inv_scale = lax.rsqrt(spread + norm_eps)
    normed = shifted * inv_scale
    return (normed * gain_vec + bias_vec, normed, inv_scale)


def norm_backward(upstream, normed, inv_scale, gain_vec):
    scaled = upstream * gain_vec
    return inv_scale * (
        scaled
        - jnp.mean(scaled, axis=-1, keepdims=True)
        - normed * jnp.mean(scaled * normed, axis=-1, keepdims=True)
    )


def gelu_value(pre_act):
    return 0.5 * pre_act * (1.0 + lax.erf(pre_act * sqrt_half))


def gelu_slope(pre_act):
    return (
        0.5 * (1.0 + lax.erf(pre_act * sqrt_half))
        + pre_act * jnp.exp(-0.5 * pre_act * pre_act) * inv_sqrt_tau
    )


def attend_forward(queries, key_rows, value_rows):
    score_scale = queries.shape[-1] ** (-0.5)

    def single_seq(seq_item):
        query_seq, key_seq, value_seq = seq_item
        scores = jnp.einsum("qhd,khd->hqk", query_seq, key_seq, precision=HIGHEST) * score_scale
        row_peak = jnp.max(scores, axis=-1, keepdims=True)
        exp_scores = jnp.exp(scores - row_peak)
        totals = jnp.sum(exp_scores, axis=-1, keepdims=True)
        context = jnp.einsum("hqk,khd->qhd", exp_scores / totals, value_seq, precision=HIGHEST)
        return (context, (row_peak + jnp.log(totals))[..., 0])

    return lax.map(single_seq, (queries, key_rows, value_rows))


def attend_backward(queries, key_rows, value_rows, context, log_totals, grad_context):
    score_scale = queries.shape[-1] ** (-0.5)

    def single_seq(seq_item):
        query_seq, key_seq, value_seq, context_seq, lse_seq, grad_seq = seq_item
        scores = jnp.einsum("qhd,khd->hqk", query_seq, key_seq, precision=HIGHEST) * score_scale
        attn_probs = jnp.exp(scores - lse_seq[..., None])
        grad_value = jnp.einsum("hqk,qhd->khd", attn_probs, grad_seq, precision=HIGHEST)
        grad_probs = jnp.einsum("qhd,khd->hqk", grad_seq, value_seq, precision=HIGHEST)
        row_dot = jnp.swapaxes(jnp.sum(grad_seq * context_seq, axis=-1), 0, 1)
        grad_scores = attn_probs * (grad_probs - row_dot[..., None]) * score_scale
        grad_query = jnp.einsum("hqk,khd->qhd", grad_scores, key_seq, precision=HIGHEST)
        grad_key = jnp.einsum("hqk,qhd->khd", grad_scores, query_seq, precision=HIGHEST)
        return (grad_query, grad_key, grad_value)

    return lax.map(single_seq, (queries, key_rows, value_rows, context, log_totals, grad_context))


def layer_forward(local_in, qkv_layer, out_layer, in_layer, down_layer, norm_set):
    full_in = gather_rows(local_in)
    rows_all = full_in.shape[0]
    width_loc = qkv_layer.shape[2]
    projected = jnp.einsum("sd,cde->cse", full_in, qkv_layer, precision=HIGHEST)
    shaped = projected.reshape(3, rows_all // LEN, LEN, width_loc // HEAD, HEAD)
    context, log_totals = attend_forward(shaped[0], shaped[1], shaped[2])
    context_rows = context.reshape(rows_all, width_loc)
    attn_part = reduce_rows(matmul(context_rows, out_layer))
    middle, normed_one, scale_one = norm_forward(
        local_in + attn_part, norm_set[0, 0], norm_set[0, 1]
    )
    full_mid = gather_rows(middle)
    pre_act = matmul(full_mid, in_layer)
    activated = gelu_value(pre_act)
    ffn_part = reduce_rows(matmul(activated, down_layer))
    result, normed_two, scale_two = norm_forward(middle + ffn_part, norm_set[1, 0], norm_set[1, 1])
    kept_set = (
        full_in,
        shaped,
        context_rows,
        log_totals,
        normed_one,
        scale_one,
        full_mid,
        pre_act,
        activated,
        normed_two,
        scale_two,
        local_in,
        middle,
    )
    return (result, kept_set)


def layer_backward(grad_top, kept_set, qkv_layer, out_layer, in_layer, down_layer, norm_set):
    (
        full_in,
        shaped,
        context_rows,
        log_totals,
        normed_one,
        scale_one,
        full_mid,
        pre_act,
        activated,
        normed_two,
        scale_two,
        local_in,
        middle,
    ) = kept_set
    rows_all = context_rows.shape[0]
    width_loc = context_rows.shape[1]
    grad_gain_two = jnp.sum(grad_top * normed_two, axis=0)
    grad_bias_two = jnp.sum(grad_top, axis=0)
    grad_second = norm_backward(grad_top, normed_two, scale_two, norm_set[1, 0])
    grad_full = gather_grads(grad_second)
    grad_act = matmul_t(grad_full, down_layer)
    grad_down = inner_rows(activated, grad_full)
    grad_pre = grad_act * gelu_slope(pre_act)
    grad_in = inner_rows(full_mid, grad_pre)
    grad_middle = grad_second + reduce_grads(matmul_t(grad_pre, in_layer))
    grad_gain_one = jnp.sum(grad_middle * normed_one, axis=0)
    grad_bias_one = jnp.sum(grad_middle, axis=0)
    grad_attn_local = norm_backward(grad_middle, normed_one, scale_one, norm_set[0, 0])
    grad_attn = gather_grads(grad_attn_local)
    grad_context = matmul_t(grad_attn, out_layer)
    grad_outw = inner_rows(context_rows, grad_attn)
    context = context_rows.reshape(shaped[0].shape)
    grad_query, grad_key, grad_value = attend_backward(
        shaped[0], shaped[1], shaped[2], context, log_totals, grad_context.reshape(shaped[0].shape)
    )
    grad_proj = jnp.stack(
        [
            grad_query.reshape(rows_all, width_loc),
            grad_key.reshape(rows_all, width_loc),
            grad_value.reshape(rows_all, width_loc),
        ]
    )
    grad_qkv = jnp.einsum("sd,cse->cde", full_in, grad_proj, precision=HIGHEST)
    grad_local = grad_attn_local + reduce_grads(
        jnp.einsum("cse,cde->sd", grad_proj, qkv_layer, precision=HIGHEST)
    )
    norm_grads = jnp.stack(
        [jnp.stack([grad_gain_one, grad_bias_one]), jnp.stack([grad_gain_two, grad_bias_two])]
    )
    return (grad_local, (grad_qkv, grad_outw, grad_in, grad_down), norm_grads)


def cut_blocks(matrix):
    leading = tuple(matrix.shape[:-2])
    row_count, col_count = matrix.shape[-2:]
    tiled = matrix.reshape(leading + (row_count // BLOCK, BLOCK, col_count // BLOCK, BLOCK))
    return jnp.swapaxes(tiled, -3, -2).reshape(-1, BLOCK, BLOCK)


def tile_blocks(qkv_part, out_part, in_part, down_part):
    return jnp.concatenate(
        [cut_blocks(qkv_part), cut_blocks(out_part), cut_blocks(in_part), cut_blocks(down_part)],
        axis=0,
    )


def join_blocks(blocks, target_shape):
    leading = tuple(target_shape[:-2])
    row_count, col_count = target_shape[-2:]
    tiled = blocks.reshape(leading + (row_count // BLOCK, col_count // BLOCK, BLOCK, BLOCK))
    return jnp.swapaxes(tiled, -3, -2).reshape(target_shape)


def untile_blocks(blocks, shape_list):
    pieces = []
    offset = 0
    for target_shape in shape_list:
        block_count = math.prod(target_shape) // (BLOCK * BLOCK)
        pieces.append(join_blocks(blocks[offset : offset + block_count], target_shape))
        offset = offset + block_count
    return pieces


def on_device(
    inputs,
    cotangent,
    loss_mask,
    keep_mask,
    w_qkv,
    w_out,
    w_in,
    w_down,
    norm_params,
    norm_moments,
    left_stats,
    right_stats,
    left_roots,
    right_roots,
):
    rows_loc = inputs.shape[0]
    seqs_loc = keep_mask.shape[0]
    row_index = lax.axis_index("mp") * rows_loc + jnp.arange(rows_loc, dtype=jnp.int32)
    seq_ids = row_index // LEN
    matches = seq_ids[:, None] == jnp.arange(seqs_loc, dtype=jnp.int32)[None, :]
    keep_rows = jnp.sum(jnp.where(matches, keep_mask[None, :], 0), axis=1).astype(jnp.float32)[
        :, None
    ]
    first_out, kept_one = layer_forward(
        inputs, w_qkv[0], w_out[0], w_in[0], w_down[0], norm_params[0]
    )
    second, kept_two = layer_forward(
        first_out, w_qkv[1], w_out[1], w_in[1], w_down[1], norm_params[1]
    )
    outputs = first_out + keep_rows * (second - first_out)
    masked_grad = cotangent * loss_mask.astype(jnp.float32)[:, None]
    grad_two, weights_two, norms_two = layer_backward(
        keep_rows * masked_grad, kept_two, w_qkv[1], w_out[1], w_in[1], w_down[1], norm_params[1]
    )
    blocks_two = tile_blocks(*weights_two)
    grad_first = (1.0 - keep_rows) * masked_grad + grad_two
    in_grads, weights_one, norms_one = layer_backward(
        grad_first, kept_one, w_qkv[0], w_out[0], w_in[0], w_down[0], norm_params[0]
    )
    blocks_one = tile_blocks(*weights_one)
    reduced = lax.psum_scatter(
        jnp.stack([blocks_one, blocks_two]), "dp", scatter_dimension=1, tiled=True
    )
    norm_grads = lax.psum(jnp.stack([norms_one, norms_two]), ("dp", "mp"))
    per_owner = reduced.shape[1]
    block_grads = reduced.reshape(-1, BLOCK, BLOCK)
    current = jnp.stack(
        [
            tile_blocks(w_qkv[0], w_out[0], w_in[0], w_down[0]),
            tile_blocks(w_qkv[1], w_out[1], w_in[1], w_down[1]),
        ]
    )
    owner_blocks = lax.dynamic_slice_in_dim(
        current, lax.axis_index("dp") * per_owner, per_owner, 1
    ).reshape(-1, BLOCK, BLOCK)
    left_new = stat_decay * left_stats + (1.0 - stat_decay) * jnp.einsum(
        "nij,nkj->nik", block_grads, block_grads, precision=HIGHEST
    )
    right_new = stat_decay * right_stats + (1.0 - stat_decay) * jnp.einsum(
        "nji,njk->nik", block_grads, block_grads, precision=HIGHEST
    )
    right_side = jnp.einsum("nij,njk->nik", block_grads, right_roots, precision=HIGHEST)
    precond = jnp.einsum("nij,njk->nik", left_roots, right_side, precision=HIGHEST)
    renewed = owner_blocks - shampoo_rate * precond * lax.rsqrt(
        jnp.mean(precond * precond, axis=(1, 2), keepdims=True) + graft_eps
    )
    everywhere = lax.all_gather(renewed.reshape(reduced.shape), "dp", axis=1, tiled=True)
    shape_list = [
        tuple(w_qkv.shape[1:]),
        tuple(w_out.shape[1:]),
        tuple(w_in.shape[1:]),
        tuple(w_down.shape[1:]),
    ]
    layer_one = untile_blocks(everywhere[0], shape_list)
    layer_two = untile_blocks(everywhere[1], shape_list)
    qkv_new = jnp.stack([layer_one[0], layer_two[0]])
    out_new = jnp.stack([layer_one[1], layer_two[1]])
    in_new = jnp.stack([layer_one[2], layer_two[2]])
    down_new = jnp.stack([layer_one[3], layer_two[3]])
    moments_new = moment_decay * norm_moments + (1.0 - moment_decay) * norm_grads * norm_grads
    norms_new = norm_params - vector_rate * norm_grads / (jnp.sqrt(moments_new) + vector_eps)
    return (
        outputs,
        in_grads,
        block_grads,
        left_new,
        right_new,
        qkv_new,
        out_new,
        in_new,
        down_new,
        norm_grads,
        moments_new,
        norms_new,
    )


HIGH = lax.Precision.HIGH
FINE = ("e", "c", "mh", "ml")
FLIP = [(0, 1), (1, 0)]
MESH_ID = pl.DeviceIdType.MESH
NN = (((1,), (0,)), ((), ()))
NT = (((1,), (1,)), ((), ()))
TN = (((0,), (0,)), ((), ()))
F32 = jnp.float32
BF16 = jnp.bfloat16
VMEM_BYTES = 60 * 2**20


def dot(left_op, right_op, dims):
    return lax.dot_general(left_op, right_op, dims, precision=HIGH, preferred_element_type=F32)


def dot16(left_op, right_op, dims):
    return lax.dot_general(left_op, right_op, dims, preferred_element_type=F32)


def halves(value):
    high = value.astype(BF16)
    return high, (value - high.astype(F32)).astype(BF16)


class Pair:
    def __init__(self, full, part, core_in, chip_in, send, recv):
        self.full, self.part, self.core_in, self.chip_in = full, part, core_in, chip_in
        self.send, self.recv = send, recv
        self.rows = full.shape[0] // 4
        self.half = self.rows // 2
        self.core = {"c": 1 - lax.axis_index("c")}
        self.chip = {"ml": 1 - lax.axis_index("ml")}
        r, h = self.rows, self.half
        self.z = [self._copy(full, i * h, full, 2 * r + i * r, h, i, self.chip) for i in range(2)]
        self.own = self._copy(full, 0, full, r, r, 2, self.core)
        self.fwd = [
            self._copy(full, 2 * r + i * r, full, 2 * r + i * r + h, h, 3 + i, self.core) for i in range(2)
        ]
        self.back = self._copy(part, r, core_in, 0, r, 5, self.core)
        self.side = [
            self._copy(part, 2 * r + i * r + h, core_in, r + i * h, h, 6 + i, self.core) for i in range(2)
        ]
        self.home = [self._copy(part, 2 * r + i * r, chip_in, i * h, h, 8 + i, self.chip) for i in range(2)]

    def _copy(self, src, src_row, dst, dst_row, count, slot, device):
        return pltpu.make_async_remote_copy(
            src_ref=src.at[pl.ds(src_row, count)],
            dst_ref=dst.at[pl.ds(dst_row, count)],
            send_sem=self.send.at[slot],
            recv_sem=self.recv.at[slot],
            device_id=device,
            device_id_type=MESH_ID,
        )

    def devices(self):
        return [self.core, self.chip]

    def start(self):
        for copy in (self.z[0], self.own, self.z[1]):
            copy.start()

    def arrive(self, tile):
        if tile == 1:
            self.own.wait_recv()
        elif tile >= 2:
            self.z[tile - 2].wait_recv()
            self.fwd[tile - 2].start()
            self.fwd[tile - 2].wait_recv()

    def reduce(self, tile):
        if tile == 1:
            self.back.start()
        elif tile >= 2:
            i, r, h = tile - 2, self.rows, self.half
            self.side[i].start()
            self.side[i].wait_recv()
            mine = pl.ds(2 * r + i * r, h)
            self.part[mine] = self.part[mine] + self.core_in[pl.ds(r + i * h, h)]
            self.home[i].start()

    def finish(self):
        self.back.wait_recv()
        for copy in self.home:
            copy.wait_recv()
        for copy in (*self.z, self.own, *self.fwd, self.back, *self.side, *self.home):
            copy.wait_send()

    def total(self):
        r = self.rows
        return self.part[:r] + self.core_in[:r] + self.chip_in[...]


PAIR_SLOTS = 10


def beside(e, mask):
    y, x = e // 2, e % 2
    return 2 * (1 - y if mask >= 2 else y) + (1 - x if mask % 2 else x)


def is_away():
    return lax.axis_index("c") != lax.axis_index("mh")


def partner_id():
    return {"c": 1 - lax.axis_index("c"), "mh": 1 - lax.axis_index("mh")}


class Fetch:
    def __init__(self, owned, foreign, send, recv):
        self.owned, self.foreign, self.send, self.recv = owned, foreign, send, recv
        self.e = lax.axis_index("e")
        self.near = [{"e": beside(self.e, mask)} for mask in (1, 2, 3)]

    def _piece(self, ref):
        count = ref.shape[-2] // 4
        rows = pl.ds(pl.multiple_of(self.e * count, count), count)
        return ref.at[:, rows] if len(ref.shape) == 3 else ref.at[rows]

    def _copy(self, job, hop):
        target = self._piece(self.foreign[job])
        return pltpu.make_async_remote_copy(
            src_ref=self._piece(self.owned[job]) if hop == 0 else target,
            dst_ref=target,
            send_sem=self.send.at[4 * job + hop],
            recv_sem=self.recv.at[4 * job + hop],
            device_id=partner_id() if hop == 0 else self.near[hop - 1],
            device_id_type=MESH_ID,
        )

    def devices(self):
        return [partner_id(), *self.near]

    def cross(self):
        @pl.when(is_away())
        def _():
            for job in range(len(self.owned)):
                self._copy(job, 0).start()

    def spread(self, job):
        @pl.when(is_away())
        def _():
            self._copy(job, 0).wait_recv()
            for hop in (1, 2, 3):
                self._copy(job, hop).start()

    def finish(self):
        @pl.when(is_away())
        def _():
            for job in range(len(self.owned)):
                for hop in (1, 2, 3):
                    self._copy(job, hop).wait_recv()
                for hop in range(4):
                    self._copy(job, hop).wait_send()


class Swap:
    def __init__(self, sources, targets, send, recv, first):
        self.sources, self.targets, self.send, self.recv, self.first = sources, targets, send, recv, first

    def _away(self, i):
        return pltpu.make_async_remote_copy(
            src_ref=self.sources[i],
            dst_ref=self.targets[i],
            send_sem=self.send.at[self.first + i],
            recv_sem=self.recv.at[self.first + i],
            device_id=partner_id(),
            device_id_type=MESH_ID,
        )

    def _here(self, i):
        return pltpu.make_async_copy(self.sources[i], self.targets[i], self.send.at[self.first + i])

    def start(self):
        for i in range(len(self.sources)):
            pl.when(is_away())(lambda: self._away(i).start())
            pl.when(jnp.logical_not(is_away()))(lambda: self._here(i).start())

    def finish(self):
        for i in range(len(self.sources)):
            pl.when(is_away())(lambda: self._away(i).wait())
            pl.when(jnp.logical_not(is_away()))(lambda: self._here(i).wait())


def chosen(order, e):
    value = order[0]
    for i in range(1, len(order)):
        value = jnp.where(e == i, order[i], value)
    return value


ATT_ORDER, ATT_CHIP, ATT_UNIT = (0, 3, 1, 2), (0, 2, 3, 1), 0
FFN_ORDER, FFN_CHIP, FFN_UNIT = (2, 0, 1, 3), (1, 2, 0, 3), 8
UNITS = 3


class PlaneSum:
    def __init__(self, grads, got, order, send, recv):
        self.grads, self.got, self.order, self.send, self.recv = grads, got, order, send, recv
        self.e = lax.axis_index("e")
        self.count = got.shape[1]
        self.copies = [self._copy(mask) for mask in (1, 2, 3)]

    def _copy(self, mask):
        there = beside(self.e, mask)
        rows = pl.ds(pl.multiple_of(chosen(self.order, there) * self.count, self.count), self.count)
        return pltpu.make_async_remote_copy(
            src_ref=self.grads.at[rows],
            dst_ref=self.got.at[mask - 1],
            send_sem=self.send.at[mask - 1],
            recv_sem=self.recv.at[mask - 1],
            device_id={"e": there},
            device_id_type=MESH_ID,
        )

    def start(self):
        for copy in self.copies:
            copy.start()

    def finish(self):
        for copy in self.copies:
            copy.wait()


class OwnerSend:
    def __init__(self, grads, got, acc, owned, order, chip, unit, send, recv, loads):
        self.acc, self.owned, self.chip, self.unit = acc, owned, chip, unit
        self.send, self.recv, self.loads = send, recv, loads
        self.e, self.c, self.mh = lax.axis_index("e"), lax.axis_index("c"), lax.axis_index("mh")
        self.count = got.shape[1]
        self.per = self.count // BLOCK
        piece = chosen(order, self.e)
        rows = pl.ds(pl.multiple_of(piece * self.count, self.count), self.count)
        self.first = unit + piece * self.per
        sources = [grads.at[rows]] + [got.at[i] for i in range(3)]
        self.reads = [pltpu.make_async_copy(sources[i], acc.at[i], loads.at[i]) for i in range(4)]

    def begin(self):
        for read in self.reads:
            read.start()

    def _unit(self, k):
        b = self.first + k
        e, c, slot = b // (2 * UNITS), (b // UNITS) % 2, b % UNITS
        here = jnp.logical_and(jnp.logical_and(e == self.e, c == self.c), self.c == self.mh)
        source = self.acc.at[0, pl.ds(k * BLOCK, BLOCK)]
        target = self.owned.at[self.mh, pl.ds(pl.multiple_of(slot * BLOCK, BLOCK), BLOCK)]
        remote = pltpu.make_async_remote_copy(
            src_ref=source,
            dst_ref=target,
            send_sem=self.send.at[k],
            recv_sem=self.recv.at[self.mh * UNITS + slot],
            device_id={"e": e, "c": c, "mh": self.c},
            device_id_type=MESH_ID,
        )
        return here, remote, pltpu.make_async_copy(source, target, self.send.at[k])

    def ship(self):
        for read in self.reads:
            read.wait()
        self.acc[0] = self.acc[0] + self.acc[1] + self.acc[2] + self.acc[3]
        for k in range(self.per):
            here, remote, local = self._unit(k)
            pl.when(here)(local.start)
            pl.when(jnp.logical_not(here))(remote.start)

    def finish(self):
        for k in range(self.per):
            here, remote, local = self._unit(k)
            pl.when(here)(local.wait)
            pl.when(jnp.logical_not(here))(remote.wait_send)
        first = UNITS * (2 * self.e + self.c)
        for mh in range(2):
            for slot in range(UNITS):
                b = first + slot
                mine = b >= FFN_UNIT if self.unit == FFN_UNIT else b < FFN_UNIT
                origin = chosen(self.chip, (b - self.unit) // self.per)
                here = jnp.logical_and(origin == self.e, jnp.logical_and(self.mh == self.c, self.mh == mh))
                piece = self.owned.at[mh, pl.ds(slot * BLOCK, BLOCK)]
                wait = pltpu.make_async_remote_copy(
                    src_ref=piece,
                    dst_ref=piece,
                    send_sem=self.send.at[0],
                    recv_sem=self.recv.at[mh * UNITS + slot],
                    device_id={"c": 1 - self.c},
                    device_id_type=MESH_ID,
                )
                pl.when(jnp.logical_and(mine, jnp.logical_not(here)))(wait.wait_recv)


def near_chips():
    return [{"e": beside(lax.axis_index("e"), mask)} for mask in (1, 2, 3)]


def sixteen():
    e, c, mh = (lax.axis_index(axis) for axis in ("e", "c", "mh"))
    devices = []
    for mask in range(4):
        for flip_c in range(2):
            for flip_h in range(2):
                if mask or flip_c or flip_h:
                    devices.append(
                        {"e": beside(e, mask), "c": 1 - c if flip_c else c, "mh": 1 - mh if flip_h else mh}
                    )
    return devices


class PlaneGather:
    def __init__(self, rows, whole, send, recv, sem):
        self.rows, self.whole, self.send, self.recv = rows, whole, send, recv
        self.e, self.c = lax.axis_index("e"), lax.axis_index("c")
        self.count = rows.shape[0]
        self.half = rows.shape[1] // 2
        self.local = pltpu.make_async_copy(rows, self._at(0, self.c), sem)
        half = self.half
        self.first = [self._copy(rows.at[:, pl.ds(i * half, half)], self._at(0, self.c, i), i, i + 1) for i in range(2)]
        self.second = []
        for i in range(2):
            near, far = i + 1, 2 - i
            self.second.append(self._copy(rows.at[:, pl.ds(i * half, half)], self._at(0, self.c, i), 2 + 2 * i, far))
            place = self._at(near, self.c, i)
            self.second.append(self._copy(place, place, 3 + 2 * i, far))
        self.core = []
        for mask in range(4):
            place = self._at(mask, self.c)
            self.core.append(self._copy(rows if mask == 0 else place, place, 6 + mask, 0))

    def _at(self, mask, c, part=None):
        owner = 2 * beside(self.e, mask) + c
        span = pl.ds(pl.multiple_of(owner * self.count, self.count), self.count)
        return self.whole.at[span] if part is None else self.whole.at[span, pl.ds(part * self.half, self.half)]

    def _copy(self, source, target, slot, mask):
        return pltpu.make_async_remote_copy(
            src_ref=source,
            dst_ref=target,
            send_sem=self.send.at[slot],
            recv_sem=self.recv.at[slot],
            device_id={"e": beside(self.e, mask)} if mask else {"c": 1 - self.c},
            device_id_type=MESH_ID,
        )

    def start(self):
        self.local.start()
        for copy in (*self.first, self.second[0], self.second[2], self.core[0]):
            copy.start()

    def middle(self):
        for i in range(2):
            self.first[i].wait_recv()
            self.second[2 * i + 1].start()

    def finish(self):
        for i in range(2):
            self.second[2 * i].wait_recv()
        self.second[1].wait_recv()
        self.second[3].wait_recv()
        for mask in (1, 2, 3):
            self.core[mask].start()
        self.local.wait()
        for copy in self.core:
            copy.wait_recv()
        for copy in (*self.first, *self.second, *self.core):
            copy.wait_send()


def greet(always, if_away):
    barrier = pltpu.get_barrier_semaphore()

    def signal(devices):
        for device in devices:
            pl.semaphore_signal(barrier, inc=1, device_id=device, device_id_type=MESH_ID)

    signal(always)

    @pl.when(is_away())
    def _():
        signal(if_away)
        pl.semaphore_wait(barrier, len(always) + len(if_away))

    if always:

        @pl.when(jnp.logical_not(is_away()))
        def _():
            pl.semaphore_wait(barrier, len(always))


def load_quarter(owned, foreign, target, sem):
    pl.when(is_away())(lambda: pltpu.make_async_copy(foreign, target, sem).start())
    pl.when(jnp.logical_not(is_away()))(lambda: pltpu.make_async_copy(owned, target, sem).start())
    return pltpu.make_async_copy(owned, target, sem)


def move_scratch(count):
    return [pltpu.SemaphoreType.DMA((count,)), pltpu.SemaphoreType.DMA((count,))]


def own_scratch(rows, width):
    return move_scratch(3) + [
        pltpu.SemaphoreType.DMA((4,)), pltpu.SemaphoreType.DMA((2 * UNITS,)), pltpu.SemaphoreType.DMA((4,)),
        pltpu.VMEM((4, rows, width), F32),
    ]


def pair_scratch(rows, width):
    return [
        pltpu.VMEM((4 * rows, width), F32),
        pltpu.VMEM((4 * rows, width), F32),
        pltpu.VMEM((2 * rows, width), F32),
        pltpu.VMEM((rows, width), F32),
        pltpu.SemaphoreType.DMA((PAIR_SLOTS,)),
        pltpu.SemaphoreType.DMA((PAIR_SLOTS,)),
    ]


VM = pl.BlockSpec(memory_space=pltpu.VMEM)
HB = pl.BlockSpec(memory_space=pl.ANY)


def shape(*dims):
    return jax.ShapeDtypeStruct(dims, F32)


def fetch(sources, targets, sems, first=0):
    copies = []
    for i, (source, target) in enumerate(zip(sources, targets)):
        copies.append(pltpu.make_async_copy(source, target, sems.at[first + i]))
        copies[-1].start()
    return copies


def tile_rows(tile, rows):
    return pl.ds(tile * rows, rows)


def ln_out(value, norm_ref, result, normed_ref, scale_ref):
    out, normed, scale = norm_forward(value, norm_ref[0:1], norm_ref[1:2])
    result[...] = out
    normed_ref[...] = normed
    scale_ref[...] = jnp.broadcast_to(scale, scale_ref.shape)


def open_kernel(rows_hbm, qkv_hbm, out_hbm, own_hbm, f_qkv, f_out, send, recv):
    job = Fetch((qkv_hbm.at[0], out_hbm.at[0]), (f_qkv, f_out), send, recv)
    swap = Swap((rows_hbm,), (own_hbm,), send, recv, 8)
    greet([], job.devices())
    job.cross()
    swap.start()
    job.spread(0)
    job.spread(1)
    swap.finish()
    job.finish()


def open_step(rows, w_qkv, w_out, collective):
    return pl.pallas_call(
        open_kernel,
        out_shape=(shape(*rows.shape), shape(*w_qkv.shape[1:]), shape(*w_out.shape[1:])),
        in_specs=[HB] * 3,
        out_specs=(HB,) * 3,
        scratch_shapes=move_scratch(9),
        compiler_params=pltpu.CompilerParams(collective_id=collective, has_side_effects=True),
        name="open_step",
    )(rows, w_qkv, w_out)


def ffn_fwd_kernel(
    layer, last,
    own_ref, norm_ref, in_hbm, down_hbm, f_in, f_down, extra_a, extra_b,
    result, normed_ref, scale_ref, full_hbm, pre_hbm, cdf_hbm, got_a, got_b,
    full, part, core_in, chip_in, send, recv, w_in, w_down, pre, cdf, sems, move_send, move_recv,
):
    pair = Pair(full, part, core_in, chip_in, send, recv)
    rows = pair.rows
    if last:
        job = Swap((extra_a, extra_b), (got_a, got_b), move_send, move_recv, 0)
        others = [partner_id()]
    else:
        job = Fetch((extra_a.at[layer + 1], extra_b.at[layer + 1]), (got_a, got_b), move_send, move_recv)
        others = job.devices()
    loads = [
        load_quarter(in_hbm.at[layer], f_in, w_in, sems.at[0]),
        load_quarter(down_hbm.at[layer], f_down, w_down, sems.at[1]),
    ]
    full[:rows] = own_ref[...]
    greet(pair.devices(), others)
    pair.start()
    if last:
        job.start()
    else:
        job.cross()
    loads[0].wait()
    stores = []
    for tile in range(4):
        span = tile_rows(tile, rows)
        pair.arrive(tile)
        if tile >= 2 and not last:
            job.spread(tile - 2)
        pre_act = dot(full[span], w_in[...], NN)
        if tile == 0:
            loads[1].wait()
        gate = 0.5 * (1.0 + lax.erf(pre_act * sqrt_half))
        pre[span] = pre_act
        cdf[span] = gate
        part[span] = dot(pre_act * gate, w_down[...], NN)
        pair.reduce(tile)
        stores += fetch(
            (full.at[span], pre.at[span], cdf.at[span]),
            (full_hbm.at[span], pre_hbm.at[span], cdf_hbm.at[span]),
            sems,
            2 + 3 * tile,
        )
    pair.finish()
    ln_out(own_ref[...] + pair.total(), norm_ref, result, normed_ref, scale_ref)
    job.finish()
    for copy in stores:
        copy.wait()


def ffn_fwd(own, w_in, w_down, f_in, f_down, extra, norm, layer, last):
    rows, width = own.shape
    hidden = w_in.shape[2]
    got = [shape(*(v.shape if last else v.shape[1:])) for v in extra]
    result, normed, scale, full, pre, cdf, *got = pl.pallas_call(
        functools.partial(ffn_fwd_kernel, layer, last),
        out_shape=(
            shape(rows, width), shape(rows, width), shape(rows, 128),
            shape(4 * rows, width), shape(4 * rows, hidden), shape(4 * rows, hidden), *got,
        ),
        in_specs=[VM, VM] + [HB] * 6,
        out_specs=(VM, VM, VM, HB, HB, HB, HB, HB),
        scratch_shapes=pair_scratch(rows, width) + [
            pltpu.VMEM(w_in.shape[1:], F32), pltpu.VMEM(w_down.shape[1:], F32),
            pltpu.VMEM((4 * rows, hidden), F32), pltpu.VMEM((4 * rows, hidden), F32),
            pltpu.SemaphoreType.DMA((14,)),
        ] + move_scratch(8),
        compiler_params=pltpu.CompilerParams(
            collective_id=4 * layer + 1, has_side_effects=True, vmem_limit_bytes=VMEM_BYTES
        ),
        name="ffn_fwd",
    )(own, norm, w_in, w_down, f_in, f_down, *extra)
    return result, (full, pre, cdf, normed, scale), got


def ln_back(grad, normed_ref, scale_ref, norm_ref, norm_grad):
    normed = normed_ref[...]
    norm_grad[0:1] = jnp.sum(grad * normed, axis=0, keepdims=True)
    norm_grad[1:2] = jnp.sum(grad, axis=0, keepdims=True)
    return norm_backward(grad, normed, scale_ref[:, :1], norm_ref[0:1])


def ffn_bwd_kernel(
    layer,
    grad_ref, normed_ref, scale_ref, norm_ref, in_hbm, down_hbm, f_in, f_down, full_hbm, pre_hbm, cdf_hbm, *rest
):
    if layer == 0:
        sum_hbm, own_hbm, part_hbm, *rest = rest
    grad_own, norm_grad, grads_hbm, *rest = rest
    if layer == 0:
        got_hbm, owned_hbm, *rest = rest
    full, part, core_in, chip_in, send, recv, w_in, w_down, mid, pre, cdf, grads, sems, *rest = rest
    if layer == 0:
        move_send, move_recv, own_send, own_recv, own_load, acc = rest
    pair = Pair(full, part, core_in, chip_in, send, recv)
    rows = pair.rows
    hidden = w_in.shape[1]
    loads = fetch((pre_hbm, cdf_hbm, full_hbm), (pre, cdf, mid), sems)
    loads.append(load_quarter(down_hbm.at[layer], f_down, w_down, sems.at[3]))
    loads.append(load_quarter(in_hbm.at[layer], f_in, w_in, sems.at[4]))
    full[:rows] = ln_back(grad_ref[...], normed_ref, scale_ref, norm_ref, norm_grad)
    if layer == 0:
        job = PlaneSum(sum_hbm, got_hbm, ATT_ORDER, move_send, move_recv)
        ship = OwnerSend(
            own_hbm, part_hbm, acc, owned_hbm, FFN_ORDER, FFN_CHIP, FFN_UNIT, own_send, own_recv, own_load
        )
        ship.begin()
    greet([pair.chip, *(sixteen() if layer == 0 else [pair.core])], [])
    pair.start()
    if layer == 0:
        job.start()
        ship.ship()
    for copy in loads:
        copy.wait()
    for tile in range(4):
        span = tile_rows(tile, rows)
        pair.arrive(tile)
        grad_act = dot(full[span], w_down[...], NT)
        pre_act, gate = pre[span], cdf[span]
        grad_pre = grad_act * (gate + pre_act * jnp.exp(-0.5 * pre_act * pre_act) * inv_sqrt_tau)
        cdf[span] = pre_act * gate
        pre[span] = grad_pre
        part[span] = dot(grad_pre, w_in[...], NT)
        pair.reduce(tile)
    width = full.shape[1]

    @pl.loop(0, width // 256)
    def _(i):
        cols = pl.ds(pl.multiple_of(i * 256, 256), 256)
        grads[cols, :] = dot(mid[:, cols], pre[...], TN)

    @pl.loop(0, hidden // 256)
    def _(i):
        cols = pl.ds(pl.multiple_of(i * 256, 256), 256)
        target = pl.ds(pl.multiple_of(width + i * 256, 256), 256)
        grads[target, :] = dot(cdf[:, cols], full[...], TN)

    store = fetch((grads,), (grads_hbm,), sems, 5)[0]
    pair.finish()
    grad_own[...] = full[:rows] + pair.total()
    store.wait()
    if layer == 0:
        job.finish()
        ship.finish()


def to_sum_args(to_sum, to_own):
    return () if to_sum is None else (to_sum, *to_own)


def ffn_bwd(grad, kept, w_in, w_down, f_in, f_down, to_sum, to_own, norm, layer):
    full, pre, cdf, normed, scale = kept
    rows, width = grad.shape
    hidden = w_in.shape[2]
    return pl.pallas_call(
        functools.partial(ffn_bwd_kernel, layer),
        out_shape=(
            shape(rows, width), shape(2, width), shape(width + hidden, width),
            *([shape(3, to_sum.shape[0] // 4, width), shape(2, UNITS * BLOCK, width)] if layer == 0 else []),
        ),
        in_specs=[VM] * 4 + [HB] * (7 if layer else 10),
        out_specs=(VM, VM, HB) + (HB, HB) * (1 - layer),
        scratch_shapes=pair_scratch(rows, width) + [
            pltpu.VMEM(w_in.shape[1:], F32), pltpu.VMEM(w_down.shape[1:], F32),
            pltpu.VMEM((4 * rows, width), F32),
            pltpu.VMEM((4 * rows, hidden), F32), pltpu.VMEM((4 * rows, hidden), F32),
            pltpu.VMEM((width + hidden, width), F32),
            pltpu.SemaphoreType.DMA((6,)),
        ] + (own_scratch((width + hidden) // 4, width) if layer == 0 else []),
        compiler_params=pltpu.CompilerParams(
            collective_id=4 * layer + 2, has_side_effects=True, vmem_limit_bytes=VMEM_BYTES
        ),
        name="ffn_bwd",
    )(grad, normed, scale, norm, w_in, w_down, f_in, f_down, full, pre, cdf, *to_sum_args(to_sum, to_own))


def attend_fwd_kernel(
    layer,
    own_ref, norm_ref, qkv_hbm, out_hbm, f_qkv, f_out, in_hbm, down_hbm,
    result, normed_ref, scale_ref, full_hbm, proj_hbm, ctx_hbm, lse_hbm, f_in, f_down,
    full, part, core_in, chip_in, send, recv, w_qkv, w_out, proj, ctx, lse, keys, values, sems, move_send, move_recv,
):
    pair = Pair(full, part, core_in, chip_in, send, recv)
    rows = pair.rows
    heads = w_out.shape[0] // HEAD
    job = Fetch((in_hbm.at[layer], down_hbm.at[layer]), (f_in, f_down), move_send, move_recv)
    loads = [
        load_quarter(qkv_hbm.at[layer], f_qkv, w_qkv, sems.at[0]),
        load_quarter(out_hbm.at[layer], f_out, w_out, sems.at[1]),
    ]
    full[:rows] = own_ref[...]
    greet(pair.devices(), job.devices())
    pair.start()
    job.cross()
    loads[0].wait()
    stores = []
    for tile in range(4):
        span = tile_rows(tile, rows)
        pair.arrive(tile)
        for part_id in range(3):
            proj[part_id, span] = dot(full[span], w_qkv[part_id], NT)
        for head in range(heads):
            cols = slice(head * HEAD, (head + 1) * HEAD)
            high, low = halves(proj[1, span, cols])
            keys[head, span] = jnp.concatenate([high, low, high], axis=1)
            high, low = halves(proj[2, span, cols])
            values[head, span] = jnp.concatenate([high, low], axis=1)
        stores += fetch((full.at[span],), (full_hbm.at[span],), sems, 2 + tile)
    stores += fetch((proj,), (proj_hbm,), sems, 6)
    job.spread(0)
    loads[1].wait()
    lanes = lax.broadcasted_iota(jnp.int32, (rows, 128), 1)
    for tile in (2, 3, 1, 0):
        span = tile_rows(tile, rows)
        sums = jnp.zeros((rows, 128), F32)
        for head in range(heads):
            cols = slice(head * HEAD, (head + 1) * HEAD)
            high, low = halves(proj[0, span, cols] * (HEAD ** -0.5))
            scores = dot16(jnp.concatenate([high, high, low], axis=1), keys[head], NT)
            peak = jnp.max(scores, axis=1, keepdims=True)
            exps = jnp.exp(scores - peak)
            totals = jnp.sum(exps, axis=1, keepdims=True)
            high, low = halves(exps)
            mixed = dot16(high, values[head], NN)
            rest = dot16(low, values[head, :, :HEAD], NN)
            ctx[span, cols] = (mixed[:, :HEAD] + mixed[:, HEAD:] + rest) / totals
            sums = jnp.where(lanes == head, peak + jnp.log(totals), sums)
        lse[span] = sums
        part[span] = dot(ctx[span], w_out[...], NN)
        pair.reduce(tile)
        if tile == 3:
            job.spread(1)
    stores += fetch((ctx, lse), (ctx_hbm, lse_hbm), sems, 7)
    pair.finish()
    ln_out(own_ref[...] + pair.total(), norm_ref, result, normed_ref, scale_ref)
    job.finish()
    for copy in stores:
        copy.wait()


def attend_fwd(own, w_qkv, w_out, f_qkv, f_out, w_in, w_down, norm, layer):
    rows, width = own.shape
    inner = w_out.shape[1]
    heads = inner // HEAD
    result, normed, scale, full, proj, ctx, lse, f_in, f_down = pl.pallas_call(
        functools.partial(attend_fwd_kernel, layer),
        out_shape=(
            shape(rows, width), shape(rows, width), shape(rows, 128),
            shape(4 * rows, width), shape(3, 4 * rows, inner), shape(4 * rows, inner), shape(4 * rows, 128),
            shape(*w_in.shape[1:]), shape(*w_down.shape[1:]),
        ),
        in_specs=[VM, VM] + [HB] * 6,
        out_specs=(VM, VM, VM) + (HB,) * 6,
        scratch_shapes=pair_scratch(rows, width) + [
            pltpu.VMEM(w_qkv.shape[1:], F32), pltpu.VMEM(w_out.shape[1:], F32),
            pltpu.VMEM((3, 4 * rows, inner), F32), pltpu.VMEM((4 * rows, inner), F32),
            pltpu.VMEM((4 * rows, 128), F32),
            pltpu.VMEM((heads, 4 * rows, 3 * HEAD), BF16), pltpu.VMEM((heads, 4 * rows, 2 * HEAD), BF16),
            pltpu.SemaphoreType.DMA((9,)),
        ] + move_scratch(8),
        compiler_params=pltpu.CompilerParams(
            collective_id=4 * layer, has_side_effects=True, vmem_limit_bytes=VMEM_BYTES
        ),
        name="attend_fwd",
    )(own, norm, w_qkv, w_out, f_qkv, f_out, w_in, w_down)
    return result, (full, proj, ctx, lse, normed, scale), (f_in, f_down)


def attend_bwd_kernel(
    layer,
    grad_ref, normed_ref, scale_ref, norm_ref, qkv_hbm, out_hbm, f_qkv, f_out, full_hbm, proj_hbm, ctx_hbm, lse_hbm,
    sum_hbm, own_hbm, part_hbm,
    grad_own, norm_grad, grads_hbm, got_hbm, owned_hbm,
    full, part, core_in, chip_in, send, recv,
    w_qkv, w_out, mid, proj, ctx, lse, gctx, dots, dproj, back_t, grads, sems,
    move_send, move_recv, own_send, own_recv, own_load, acc,
):
    pair = Pair(full, part, core_in, chip_in, send, recv)
    rows = pair.rows
    inner = w_out.shape[0]
    heads = inner // HEAD
    loads = fetch((ctx_hbm, proj_hbm, lse_hbm, full_hbm), (ctx, proj, lse, mid), sems)
    loads.append(load_quarter(out_hbm.at[layer], f_out, w_out, sems.at[4]))
    loads.append(load_quarter(qkv_hbm.at[layer], f_qkv, w_qkv, sems.at[5]))
    full[:rows] = ln_back(grad_ref[...], normed_ref, scale_ref, norm_ref, norm_grad)
    job = PlaneSum(sum_hbm, got_hbm, FFN_ORDER, move_send, move_recv)
    if layer == 0:
        ship = OwnerSend(
            own_hbm, part_hbm, acc, owned_hbm, ATT_ORDER, ATT_CHIP, ATT_UNIT, own_send, own_recv, own_load
        )
        ship.begin()
    greet([pair.chip, *(sixteen() if layer == 0 else [pair.core, *near_chips()])], [])
    pair.start()
    if layer == 0:
        ship.ship()
    job.start()
    for copy in loads:
        copy.wait()
    lanes = lax.broadcasted_iota(jnp.int32, (rows, 128), 1)
    for tile in range(4):
        span = tile_rows(tile, rows)
        pair.arrive(tile)
        grad_ctx = dot(full[span], w_out[...], NT)
        gctx[span] = grad_ctx
        products = grad_ctx * ctx[span]
        sums = jnp.zeros((rows, 128), F32)
        for head in range(heads):
            cols = slice(head * HEAD, (head + 1) * HEAD)
            sums = jnp.where(lanes == head, jnp.sum(products[:, cols], axis=1, keepdims=True), sums)
        dots[span] = sums
    block = 2 * rows
    for head in range(heads):
        cols = slice(head * HEAD, (head + 1) * HEAD)
        key_high, key_low = halves(proj[1, :, cols])
        keys = jnp.concatenate([key_high, key_low, key_high], axis=1)
        keys_two = jnp.concatenate([key_high, key_low], axis=1)
        high, low = halves(proj[2, :, cols])
        values = jnp.concatenate([high, low, high], axis=1)
        for step in range(2):
            span = pl.ds(step * block, block)
            query = proj[0, span, cols] * (HEAD ** -0.5)
            high, low = halves(query)
            scores = dot16(jnp.concatenate([high, high, low], axis=1), keys, NT)
            probs = jnp.exp(scores - lse[span, head:head + 1])
            upstream = gctx[span, cols]
            high, low = halves(upstream)
            grad_probs = dot16(jnp.concatenate([high, high, low], axis=1), values, NT)
            grad_scores = probs * (grad_probs - dots[span, head:head + 1])
            prob_high, prob_low = halves(probs)
            up_high, up_low = halves(upstream.T)
            mixed = dot16(jnp.concatenate([up_high, up_low], axis=0), prob_high, NN)
            grad_v = mixed[:HEAD] + mixed[HEAD:] + dot16(up_high, prob_low, NN)
            score_high, score_low = halves(grad_scores)
            q_high, q_low = halves(query.T)
            mixed = dot16(jnp.concatenate([q_high, q_low], axis=0), score_high, NN)
            grad_k = mixed[:HEAD] + mixed[HEAD:] + dot16(q_high, score_low, NN)
            mixed = dot16(score_high, keys_two, NN)
            grad_q = mixed[:, :HEAD] + mixed[:, HEAD:] + dot16(score_low, key_high, NN)
            dproj[0, span, cols] = grad_q * (HEAD ** -0.5)
            if step == 0:
                back_t[1, cols, :] = grad_k
                back_t[2, cols, :] = grad_v
            else:
                back_t[1, cols, :] = back_t[1, cols, :] + grad_k
                back_t[2, cols, :] = back_t[2, cols, :] + grad_v
        dproj[1, :, cols] = back_t[1, cols, :].T
        dproj[2, :, cols] = back_t[2, cols, :].T
    for tile in (2, 3, 1, 0):
        span = tile_rows(tile, rows)
        part[span] = (
            dot(dproj[0, span], w_qkv[0], NN) + dot(dproj[1, span], w_qkv[1], NN) + dot(dproj[2, span], w_qkv[2], NN)
        )
        pair.reduce(tile)
    half = full.shape[1] // 2
    grads[:inner] = dot(dproj[0], mid[...], TN)
    middle = dot(back_t[1], mid[...], NN)
    side = inner // 2
    grads[inner:inner + side, :half] = middle[:side, :half]
    grads[inner:inner + side, half:] = middle[side:, :half]
    grads[inner + side:2 * inner, :half] = middle[:side, half:]
    grads[inner + side:2 * inner, half:] = middle[side:, half:]
    grads[2 * inner:3 * inner] = dot(back_t[2], mid[...], NN)
    grads[3 * inner:] = dot(ctx[...], full[...], TN)
    store = fetch((grads,), (grads_hbm,), sems, 6)[0]
    pair.finish()
    grad_own[...] = full[:rows] + pair.total()
    store.wait()
    job.finish()
    if layer == 0:
        ship.finish()


def attend_bwd(grad, kept, w_qkv, w_out, f_qkv, f_out, to_sum, to_own, norm, layer):
    full, proj, ctx, lse, normed, scale = kept
    rows, width = grad.shape
    inner = w_out.shape[1]
    return pl.pallas_call(
        functools.partial(attend_bwd_kernel, layer),
        out_shape=(
            shape(rows, width), shape(2, width), shape(4 * inner, width),
            shape(3, to_sum.shape[0] // 4, width), shape(2, UNITS * BLOCK, width),
        ),
        in_specs=[VM] * 4 + [HB] * 11,
        out_specs=(VM, VM, HB, HB, HB),
        scratch_shapes=pair_scratch(rows, width) + [
            pltpu.VMEM(w_qkv.shape[1:], F32), pltpu.VMEM(w_out.shape[1:], F32),
            pltpu.VMEM((4 * rows, width), F32),
            pltpu.VMEM(proj.shape, F32), pltpu.VMEM(ctx.shape, F32), pltpu.VMEM(lse.shape, F32),
            pltpu.VMEM(ctx.shape, F32), pltpu.VMEM(lse.shape, F32), pltpu.VMEM(proj.shape, F32),
            pltpu.VMEM((3, inner, 4 * rows), F32),
            pltpu.VMEM((4 * inner, width), F32),
            pltpu.SemaphoreType.DMA((7,)),
        ] + own_scratch(inner, width),
        compiler_params=pltpu.CompilerParams(
            collective_id=4 * layer + 3, has_side_effects=True, vmem_limit_bytes=VMEM_BYTES
        ),
        name="attend_bwd",
    )(grad, normed, scale, norm, w_qkv, w_out, f_qkv, f_out, full, proj, ctx, lse, to_sum, *to_own)


def swap_partner(rows, home):
    return jnp.where(home, rows, lax.ppermute(rows, ("c", "mh"), [(1, 2), (2, 1)]))


def close_one_kernel(
    sum_hbm, own_hbm, part_hbm, rows_hbm, norm_a, norm_b, norm_c, norm_d, params, moments,
    got_hbm, owned_hbm, grad_hbm, norm_grads, moments_new, norms_new,
    move_send, move_recv, own_send, own_recv, own_load, acc, swap_send, swap_recv, norm_in, norm_send, norm_recv,
):
    job = PlaneSum(sum_hbm, got_hbm, ATT_ORDER, move_send, move_recv)
    ship = OwnerSend(own_hbm, part_hbm, acc, owned_hbm, FFN_ORDER, FFN_CHIP, FFN_UNIT, own_send, own_recv, own_load)
    swap = Swap((rows_hbm,), (grad_hbm,), swap_send, swap_recv, 0)
    ship.begin()
    for i, ref in enumerate((norm_a, norm_b, norm_c, norm_d)):
        norm_grads[2 * i:2 * i + 2] = ref[...]
    e = lax.axis_index("e")
    flips = [{axis: 1 - lax.axis_index(axis)} for axis in ("c", "ml", "mh")] + [{"e": beside(e, m)} for m in (1, 2)]
    greet([flips[1], *sixteen()], [])
    job.start()
    swap.start()
    for i, device in enumerate(flips):
        copy = pltpu.make_async_remote_copy(
            src_ref=norm_grads,
            dst_ref=norm_in.at[i],
            send_sem=norm_send.at[i],
            recv_sem=norm_recv.at[i],
            device_id=device,
            device_id_type=MESH_ID,
        )
        copy.start()
        if i == 0:
            ship.ship()
        copy.wait()
        norm_grads[...] = norm_grads[...] + norm_in[i]
    total = norm_grads[...]
    moment = moment_decay * moments[...] + (1.0 - moment_decay) * total * total
    moments_new[...] = moment
    norms_new[...] = params[...] - vector_rate * total / (jnp.sqrt(moment) + vector_eps)
    job.finish()
    swap.finish()
    ship.finish()


def close_one(to_sum, to_own, rows, norms, params, moments):
    width = rows.shape[1]
    piece = to_own[0].shape[0] // 4
    return pl.pallas_call(
        close_one_kernel,
        out_shape=(
            shape(3, to_sum.shape[0] // 4, width), shape(2, UNITS * BLOCK, width), shape(*rows.shape),
            shape(8, width), shape(8, width), shape(8, width),
        ),
        in_specs=[HB] * 4 + [VM] * 6,
        out_specs=(HB, HB, HB, VM, VM, VM),
        scratch_shapes=own_scratch(piece, width) + move_scratch(1)
        + [pltpu.VMEM((5, 8, width), F32)] + move_scratch(5),
        compiler_params=pltpu.CompilerParams(
            collective_id=9, has_side_effects=True, vmem_limit_bytes=VMEM_BYTES
        ),
        name="close_one",
    )(to_sum, *to_own, rows, *norms, params.reshape(8, width), moments.reshape(8, width))


def close_two_kernel(
    own_hbm, part_hbm, rows_hbm, owned_hbm, whole_hbm,
    own_send, own_recv, own_load, acc, move_send, move_recv, sem,
):
    ship = OwnerSend(own_hbm, part_hbm, acc, owned_hbm, ATT_ORDER, ATT_CHIP, ATT_UNIT, own_send, own_recv, own_load)
    job = PlaneGather(rows_hbm, whole_hbm, move_send, move_recv, sem)
    ship.begin()
    greet(sixteen(), [])
    ship.ship()
    job.start()
    job.middle()
    ship.finish()
    job.finish()


def close_two(to_own, rows):
    width = rows.shape[1]
    piece = to_own[0].shape[0] // 4
    return pl.pallas_call(
        close_two_kernel,
        out_shape=(shape(2, UNITS * BLOCK, width), shape(8 * rows.shape[0], width)),
        in_specs=[HB] * 3,
        out_specs=(HB, HB),
        scratch_shapes=own_scratch(piece, width)[2:] + move_scratch(10) + [pltpu.SemaphoreType.DMA],
        compiler_params=pltpu.CompilerParams(
            collective_id=10, has_side_effects=True, vmem_limit_bytes=VMEM_BYTES
        ),
        name="close_two",
    )(*to_own, rows)


def close_three_kernel(rows_hbm, whole_hbm, move_send, move_recv, sem):
    job = PlaneGather(rows_hbm, whole_hbm, move_send, move_recv, sem)
    greet([{"c": 1 - lax.axis_index("c")}, *near_chips()], [])
    job.start()
    job.middle()
    job.finish()


def close_three(rows):
    return pl.pallas_call(
        close_three_kernel,
        out_shape=shape(8 * rows.shape[0], rows.shape[1]),
        in_specs=[HB],
        out_specs=HB,
        scratch_shapes=move_scratch(10) + [pltpu.SemaphoreType.DMA],
        compiler_params=pltpu.CompilerParams(collective_id=11, has_side_effects=True),
        name="close_three",
    )(rows)


def shampoo_kernel(
    layer,
    ffn_ref, att_ref, qkv_hbm, out_hbm, in_hbm, down_hbm, left_ref, right_ref, left_root, right_root, *rest
):
    grads_ref, left_new, right_new, rows_ref, current, sems = rest[-6:]
    owner = 2 * lax.axis_index("e") + lax.axis_index("c")
    width = rows_ref.shape[1]
    half = width // 2

    def bring(source, row, col, cols, slot):
        return pltpu.make_async_copy(
            source, current.at[pl.ds(row, BLOCK), pl.ds(col, cols)], sems.at[slot]
        )

    def qkv_copies(who):
        def part(c, i, col=None):
            ref = qkv_hbm.at[layer, c, pl.ds(i * BLOCK, BLOCK)]
            return ref if col is None else qkv_hbm.at[layer, c, pl.ds(i * BLOCK, BLOCK), pl.ds(col, half)]

        mixed = 2 if who == 0 else 0
        plain = [(0, 0), (0, 1)] if who == 0 else [(2, 0), (2, 1)]
        copies = [bring(part(1, i, who * half), mixed * BLOCK, i * half, half, i) for i in range(2)]
        for n, (c, i) in enumerate(plain):
            row = (n if who == 0 else n + 1) * BLOCK
            copies.append(bring(part(c, i), row, 0, width, 2 + n))
        return copies

    def wide_copy(source, first, s):
        b = UNITS * owner + s - first
        rows = pl.ds(pl.multiple_of(b * BLOCK, BLOCK), BLOCK)
        return bring(source.at[layer, rows], s * BLOCK, 0, width, s)

    for who in range(2):

        @pl.when(owner == who)
        def _():
            copies = qkv_copies(who)
            for copy in copies:
                copy.start()
            for copy in copies:
                copy.wait()

    @pl.when(owner >= 2)
    def _():
        for s in range(UNITS):
            b = UNITS * owner + s
            pl.when(b < 8)(lambda: wide_copy(out_hbm, 6, s).start())
            pl.when(jnp.logical_and(b >= 8, b < 16))(lambda: wide_copy(in_hbm, 8, s).start())
            pl.when(b >= 16)(lambda: wide_copy(down_hbm, 16, s).start())
        for s in range(UNITS):
            bring(current.at[pl.ds(0, BLOCK)], s * BLOCK, 0, width, s).wait()

    def stripe(s, turned):
        rows = pl.ds(pl.multiple_of(s * BLOCK, BLOCK), BLOCK)
        ffn = UNITS * owner + s >= FFN_UNIT
        summed = jnp.where(ffn, ffn_ref[0, rows] + ffn_ref[1, rows], att_ref[0, rows] + att_ref[1, rows])
        old = current[rows]
        fresh = []
        for u in range(width // BLOCK):
            cols = slice(u * BLOCK, (u + 1) * BLOCK)
            tile = summed[:, cols]
            if turned:
                tile = tile.T
                across = 2 * (u % 4) + u // 4
                mixed = jnp.where(owner == 0, s == 2, s == 0)
                n = jnp.where(
                    mixed,
                    jnp.where(owner == 0, 16, 0) + across,
                    jnp.where(owner == 0, 0, 7) + 2 * u + s,
                )
            else:
                n = s * (width // BLOCK) + u
            grads_ref[n] = tile
            left_new[n] = stat_decay * left_ref[n] + (1.0 - stat_decay) * dot(tile, tile, NT)
            right_new[n] = stat_decay * right_ref[n] + (1.0 - stat_decay) * dot(tile, tile, TN)
            step = dot(left_root[n], dot(tile, right_root[n], NN), NN)
            size = jnp.mean(jnp.mean(step * step, axis=1, keepdims=True), axis=0, keepdims=True)
            step = shampoo_rate * step * lax.rsqrt(size + graft_eps)
            fresh.append(old[:, cols] - (step.T if turned else step))
        rows_ref[rows] = jnp.concatenate(fresh, axis=1)

    for turned in (True, False):

        @pl.when(owner < 2 if turned else owner >= 2)
        def _():
            @pl.loop(0, UNITS)
            def _(s):
                stripe(s, turned)


def shampoo(ffn_part, att_part, weights, stats, layer, earlier):
    width = ffn_part.shape[2]
    count = stats[0].shape[0] // 2
    block = pl.BlockSpec((count, BLOCK, BLOCK), lambda i: (layer, 0, 0))
    full = jax.ShapeDtypeStruct(stats[0].shape, F32)

    def whole(*dims):
        return pl.BlockSpec(dims, lambda i: (0,) * len(dims))

    return pl.pallas_call(
        functools.partial(shampoo_kernel, layer),
        grid=(1,),
        out_shape=(full, full, full, shape(UNITS * BLOCK, width)),
        in_specs=[whole(*ffn_part.shape), whole(*att_part.shape)] + [HB] * 4 + [block] * 4 + [HB] * len(earlier),
        out_specs=(block, block, block, whole(UNITS * BLOCK, width)),
        scratch_shapes=[pltpu.VMEM((UNITS * BLOCK, width), F32), pltpu.SemaphoreType.DMA((4,))],
        input_output_aliases={10 + i: i for i in range(len(earlier))},
        compiler_params=pltpu.CompilerParams(vmem_limit_bytes=VMEM_BYTES),
        name="shampoo",
    )(ffn_part, att_part, *weights, *stats, *earlier)


def unarrange(rows):
    half = rows.shape[1] // 2
    low, high = rows[192:288], rows[288:384]
    mid = jnp.concatenate(
        [
            jnp.concatenate([low[:, :half], high[:, :half]], axis=1),
            jnp.concatenate([low[:, half:], high[:, half:]], axis=1),
        ],
        axis=0,
    )
    return jnp.stack([rows[:192], mid, rows[384:576]]), rows[576:768], rows[768:1536], rows[1536:2304]


def on_fine(
    inputs,
    cotangent,
    loss_mask,
    keep_mask,
    w_qkv,
    w_out,
    w_in,
    w_down,
    norm_params,
    norm_moments,
    left_stats,
    right_stats,
    left_roots,
    right_roots,
):
    home = lax.axis_index("c") == lax.axis_index("mh")
    masked = cotangent * loss_mask.astype(jnp.float32)[:, None]
    flag = jnp.broadcast_to(keep_mask.astype(jnp.float32)[:, None], (8, 128))
    w_qkv = jnp.swapaxes(w_qkv, 2, 3)
    hidden, f_qkv, f_out = open_step(inputs, w_qkv, w_out, 8)
    used = []
    kept = []
    states = []
    for layer in range(2):
        middle, kept_a, (f_in, f_down) = attend_fwd(
            hidden, w_qkv, w_out, f_qkv, f_out, w_in, w_down, norm_params[layer, 0], layer
        )
        used.append((f_qkv, f_out, f_in, f_down))
        extra = (w_qkv, w_out) if layer == 0 else (masked, flag)
        hidden, kept_f, got = ffn_fwd(
            middle, w_in, w_down, f_in, f_down, extra, norm_params[layer, 1], layer, layer == 1
        )
        kept.append((kept_a, kept_f))
        states.append(hidden)
        f_qkv, f_out = got
    masked, keep = got[0], got[1][0, 0]
    outputs = swap_partner(states[0] + keep * (states[1] - states[0]), home)
    grad = keep * masked
    to_sum = to_own = None
    owned, norms = [], []
    for layer in (1, 0):
        f_qkv, f_out, f_in, f_down = used[layer]
        kept_a, kept_f = kept[layer]
        grad_mid, norm_two, g_ffn, *moved = ffn_bwd(
            grad, kept_f, w_in, w_down, f_in, f_down, to_sum, to_own, norm_params[layer, 1], layer
        )
        if layer == 0:
            owned.append(moved[1])
            to_own = (to_sum, moved[0])
        else:
            to_own = (g_ffn, g_ffn)
        grad, norm_one, g_att, got, part = attend_bwd(
            grad_mid, kept_a, w_qkv, w_out, f_qkv, f_out, g_ffn, to_own, norm_params[layer, 0], layer
        )
        if layer == 1:
            grad = (1.0 - keep) * masked + grad
        else:
            owned.append(part)
        norms = [norm_one, norm_two] + norms
        to_sum, to_own = g_att, (g_ffn, got)
    got, part, in_grads, norm_grads, moments_new, norms_new = close_one(
        to_sum, to_own, grad, norms, norm_params, norm_moments
    )
    owned.append(part)
    weights = (w_qkv, w_out, w_in, w_down)
    stats = (left_stats, right_stats, left_roots, right_roots)
    *blocks, renewed = shampoo(owned[0], owned[1], weights, stats, 1, ())
    part, second = close_two((to_sum, got), renewed)
    owned.append(part)
    *blocks, renewed = shampoo(owned[2], owned[3], weights, stats, 0, blocks)
    first = close_three(renewed)
    fresh = [jnp.stack(pair) for pair in zip(unarrange(first), unarrange(second))]
    fresh[0] = jnp.swapaxes(fresh[0], 2, 3)
    like = norm_params.shape
    return (
        outputs, in_grads, *blocks, *fresh,
        norm_grads.reshape(like), moments_new.reshape(like), norms_new.reshape(like),
    )


def fine_solution(mesh):
    n_dp, n_mp = mesh.shape["dp"], mesh.shape["mp"]
    fine = Mesh(mesh.devices.reshape(n_dp // 2, 2, n_mp // 2, 2), FINE)
    rows, part = P(FINE, None), ("mh", "ml")
    blocks = P(FINE, None, None)
    weights = (P(None, None, None, part), P(None, part, None), P(None, None, part), P(None, part, None))
    in_specs = (rows, rows, P(FINE), P(("e", "c")), *weights, P(), P(), blocks, blocks, blocks, blocks)
    out_specs = (rows, rows, blocks, blocks, blocks, *weights, P(), P(), P())
    return jax.shard_map(on_fine, mesh=fine, in_specs=in_specs, out_specs=out_specs, check_vma=False)


def solution(mesh):
    if mesh.shape["dp"] == 8 and mesh.shape["mp"] == 4:
        return fine_solution(mesh)
    return wide_solution(mesh)


def wide_solution(mesh):
    in_specs = (
        P(("dp", "mp"), None),
        P(("dp", "mp"), None),
        P(("dp", "mp")),
        P("dp"),
        P(None, None, None, "mp"),
        P(None, "mp", None),
        P(None, None, "mp"),
        P(None, "mp", None),
        P(),
        P(),
        P(("dp", "mp"), None, None),
        P(("dp", "mp"), None, None),
        P(("dp", "mp"), None, None),
        P(("dp", "mp"), None, None),
    )
    out_specs = (
        P(("dp", "mp"), None),
        P(("dp", "mp"), None),
        P(("dp", "mp"), None, None),
        P(("dp", "mp"), None, None),
        P(("dp", "mp"), None, None),
        P(None, None, None, "mp"),
        P(None, "mp", None),
        P(None, None, "mp"),
        P(None, "mp", None),
        P(),
        P(),
        P(),
    )
    return jax.shard_map(
        on_device, mesh=mesh, in_specs=in_specs, out_specs=out_specs, check_vma=False
    )
```
